256 devices in a mesh: lat: 16 (over y, x), lon: 16 (over z, core).
Axes of the slice: x: 4, y: 4, z: 8, core: 2. Of those that a mesh axis runs over, the one named last changes fastest.
Arguments:
- grid: bfloat16 [512, 4096, 128], P('lat', 'lon'), may hold values from -6 to 6
- npts: int32 [512], replicated, may hold values from 3328 to 4096, as said below
- fraction: bfloat16 [512, 4096], P('lat', 'lon'), may hold values from 0 to 1
- start: int32 [512, 4096], P('lat', 'lon'), may hold values from 0 to 124
- src_dev: int32 [16, 16, 64, 1], P('lat', 'lon'), may hold values from 0 to 15; in each aligned block of 64 rows (0 to 63, 64 to 127, ..., all dimensions but the last counted through in order) at most 8 rows name the same one
- src_sub: int32 [16, 16, 64], P('lat', 'lon'), may hold values from 0 to 1
Outputs:
- departed: bfloat16 [512, 4096, 128], P('lat', 'lon')
- fourier: float32 [512, 2, 1280, 128], P(('lat', 'lon'))
The draws below stay inside these ranges and needn't reach their ends.
Inputs may be any that keep to these rules, and one draw needn't show every extreme that they name: `npts`: each a multiple of 4; one latitude has exactly 4096 points and one exactly the least value. `src_dev`: among the 64 arrival blocks of one device no sector is named by more than 8 of them; some sector is named by exactly 8. `start`: the four stencil points lie inside the source block.
All inputs are finite; a program needn't handle non-finite values.
Results may differ from the reference program's by a relative error of at most 0.0055.
Values may be sent and summed in bfloat16 or wider, within the bound.
A program may use at most 64 MiB of HBM per device.

```python
import math
import jax
import jax.numpy as jnp
import numpy as np
from jax import lax

NLON = 4096
MMAX = 1280
LAT_DEV = 32
CH = 128
NLAT = 512
BPL = 2
NBLK = 64
SLOTS = 8
N_LAT = 16
N_LON = 16


def draw_npts(key, part):
    key = jax.random.fold_in(key, 11)
    key_cut, key_long, key_short = jax.random.split(key, 3)
    steps_most = (NLON - 2 * MMAX) // 8
    cut = jax.random.randint(key_cut, (NLAT,), 0, steps_most + 1)
    counts = NLON - 4 * cut
    longest = jax.random.randint(key_long, (), 0, NLAT)
    shortest = (longest + 1 + jax.random.randint(key_short, (), 0, NLAT - 1)) % NLAT
    counts = counts.at[longest].set(NLON).at[shortest].set(NLON - 4 * steps_most)
    return counts.astype(jnp.int32)


def plant(entries, stream_key, least, top_value):
    place = [jax.random.randint(jax.random.fold_in(stream_key, axis), (), 0, length) for axis, length in enumerate(entries.shape)]
    main_axis = entries.shape.index(max(entries.shape))
    beside = place[:main_axis] + [(place[main_axis] + 1) % entries.shape[main_axis]] + place[main_axis + 1:]
    return entries.at[tuple(place)].set(least).at[tuple(beside)].set(top_value)


def block_levels(stream_key, extent, cuts, smallest, largest):
    level = 1.0
    for position, blocks in cuts:
        draws = jax.random.uniform(jax.random.fold_in(jax.random.fold_in(stream_key, 6), position), (blocks,), jnp.float32, smallest / len(cuts), largest / len(cuts))
        level = level * jnp.repeat(jnp.exp(draws), extent[position] // blocks).reshape((-1,) + (1,) * (len(extent) - 1 - position))
    return level


def shared_out(own_key, own, number, rows, amount, top, reach, slope):
    ranking = jax.random.permutation(own_key, amount)
    crowded, common = portions_of(amount, rows * top, reach, slope, True), portions_of(amount, rows * top, reach, slope, False)
    places = jnp.arange(amount)

    def named(lengths, offset_by):
        used = int((lengths > 0).sum())
        fixed = max(1, used // 4)
        moved = fixed + (places - fixed + offset_by * (used - fixed)) % max(1, amount - fixed)
        return jnp.zeros((amount,), jnp.int32).at[ranking[jnp.where(places < fixed, places, moved)]].set(jnp.asarray(lengths, jnp.int32))

    lengths = jnp.where(number % 4 == 0, named(crowded, number // 4), named(common, number - number // 4 - 1))
    mixed = jax.random.permutation(jax.random.fold_in(own, 3), amount)
    donor, sink = mixed[0:amount // 2 * 2:2], mixed[1:amount // 2 * 2:2]
    slack = jnp.minimum(lengths[donor] - 1, reach - lengths[sink]) // 2
    slack = jnp.where((donor == ranking[0]) | (sink == ranking[0]) | (lengths[sink] == 0), 0, jnp.maximum(slack, 0))
    moved = jax.random.randint(jax.random.fold_in(own, 4), (amount // 2,), 0, 1 << 20) % (slack + 1)
    lengths = lengths.at[donor].add(-moved).at[sink].add(moved)
    items = jnp.searchsorted(jnp.cumsum(lengths), jnp.arange(rows * top), side="right").astype(jnp.int32)
    table = items.reshape(top, rows).T
    table = table[jax.random.permutation(jax.random.fold_in(own, 1), rows)]
    offset_by = jax.random.randint(jax.random.fold_in(own, 2), (rows, 1), 0, top)
    return jnp.take_along_axis(table, (jnp.arange(top)[None, :] + offset_by) % top, axis=1)


def portions_of(count, total, bound, skew, full):
    weights = [(1 << 20) // math.isqrt(grade ** skew) + 1 for grade in range(1, count + 1)]
    largest = bound if full else min(bound, max(-(-total // count), total * weights[0] // sum(weights)))
    least = 1 if total - largest >= count - 1 else 0
    given, rest = [largest] + [least] * (count - 1), total - largest - least * (count - 1)
    while rest > 0:
        candidates = [i for i in range(1, count) if given[i] < largest] or [i for i in range(1, count) if given[i] < bound]
        pool, remaining = sum([weights[i] for i in candidates]), rest
        for i in candidates:
            addition = min(bound - given[i], max(1, remaining * weights[i] // pool), rest)
            given[i] = given[i] + addition
            rest = rest - addition
    return np.array(given)


def bell_draw(own_key, shape, width, reach, cuts=(), kind=jnp.bfloat16):
    values = width * jax.random.normal(own_key, shape, jnp.float32)
    if cuts:
        values = values * block_levels(own_key, shape, cuts, -0.22, 0.18)
    return jnp.clip(values, -reach, reach).astype(kind)


def setup_inputs(seed: int = 0) -> dict:
    seeds = jax.random.split(jax.random.key(seed), 7)
    grid = bell_draw(seeds[0], (NLAT, NLON, CH), 1.0, 6.0, ((0, 16), (1, 16)))
    npts = draw_npts(jax.random.fold_in(seeds[6], 71), 0)
    fraction = jnp.clip(1.0 * jax.random.uniform(seeds[2], (NLAT, NLON), jnp.float32) ** block_levels(seeds[2], (NLAT, NLON), ((0, 16), (1, 16)), -0.2, 0.2), 0.0, 1.0).astype(jnp.bfloat16)
    start = plant(jax.random.randint(seeds[3], (NLAT, NLON), 0, 125), jax.random.fold_in(seeds[3], 1), 0, 124).astype(jnp.int32)
    src_dev_keys = jax.random.split(jax.random.fold_in(seeds[4], 1), N_LAT * N_LON * NBLK // NBLK)
    src_dev_turns = jax.random.permutation(jax.random.fold_in(seeds[4], 3), N_LAT * N_LON * NBLK // NBLK)
    src_dev = jax.vmap(lambda own, number: shared_out(jax.random.fold_in(seeds[4], 2), own, number, NBLK, N_LON, 1, SLOTS, 2))(src_dev_keys, src_dev_turns).reshape((N_LAT, N_LON, NBLK, 1))
    src_sub = plant(jax.random.randint(seeds[5], (N_LAT, N_LON, NBLK), 0, BPL), jax.random.fold_in(seeds[5], 1), 0, BPL - 1).astype(jnp.int32)
    return {"grid": grid, "npts": npts, "fraction": fraction, "start": start, "src_dev": src_dev, "src_sub": src_sub}


def cubic_weights(shifted):
    return jnp.stack([-shifted * (shifted - 1.0) * (shifted - 2.0) / 6.0, (shifted + 1.0) * (shifted - 1.0) * (shifted - 2.0) / 2.0, -(shifted + 1.0) * shifted * (shifted - 2.0) / 2.0, (shifted + 1.0) * shifted * (shifted - 1.0) / 6.0], axis=-1)

def zonal_transform(values, length):
    column_ids = jnp.arange(NLON, dtype=jnp.int32)
    wave_ids = jnp.arange(MMAX, dtype=jnp.int32)
    residue = wave_ids[:, None] * column_ids[None, :] % length
    phase = residue.astype(jnp.float32) * (jnp.float32(2.0 * math.pi) / length.astype(jnp.float32))
    cosine = jnp.dot(jnp.cos(phase), values, precision=lax.Precision.HIGHEST)
    sine = jnp.dot(-jnp.sin(phase), values, precision=lax.Precision.HIGHEST)
    return jnp.stack([cosine, sine]) / jnp.sqrt(length.astype(jnp.float32))

def reference(grid, npts, fraction, start, src_dev, src_sub):
    sub_blocks = NLON // (128 * N_LON)
    block_col = src_dev[..., 0] * sub_blocks + src_sub
    block_col = block_col.reshape(N_LAT, N_LON, LAT_DEV, sub_blocks).transpose(0, 2, 1, 3).reshape(NLAT, NLON // 128)
    first = jnp.repeat(block_col, 128, axis=1) * 128 + start
    weights = cubic_weights(fraction.astype(jnp.float32))
    column_ids = jnp.arange(NLON, dtype=jnp.int32)

    def one_latitude(items):
        row, begin, weight, length = items
        alive = (column_ids < length)[:, None]
        source = jnp.where(alive, row, jnp.zeros_like(row))
        total = jnp.zeros((NLON, CH), jnp.float32)
        for offset in range(4):
            total = total + weight[:, offset:offset + 1] * jnp.take(source, begin + offset, axis=0).astype(jnp.float32)
        moved = jnp.where(alive, total, jnp.zeros_like(total)).astype(jnp.bfloat16)
        return (moved, zonal_transform(moved.astype(jnp.float32), length))
    departed, fourier = lax.map(one_latitude, (grid, first, weights, npts))
    return (departed, fourier)
```

```python
import functools
import math

import jax
import jax.numpy as jnp
from jax import lax
from jax.experimental import pallas as pl
from jax.experimental.pallas import tpu as pltpu
from jax.sharding import PartitionSpec as P

MMAX = 1280
BLK = 128
WAVES = 128
INNER = 512
LEAST = 3328
FIX = float(1 << 24)
MESH = pl.DeviceIdType.MESH


def unit(turns):
    x = turns * math.pi
    y = x * x
    sine = x * (1.0 + y * (-1 / 6 + y * (1 / 120 + y * (-1 / 5040 + y * (1 / 362880 - y / 39916800)))))
    cosine = 1.0 + y * (
        -1 / 2 + y * (1 / 24 + y * (-1 / 720 + y * (1 / 40320 + y * (-1 / 3628800 + y / 479001600))))
    )
    return 1.0 - 2.0 * sine * sine, -2.0 * sine * cosine


def times(a, b):
    return a[0] * b[0] - a[1] * b[1], a[0] * b[1] + a[1] * b[0]


def turned(product, length, inverse):
    rest = product - jnp.round(product * inverse) * length
    return unit(rest * inverse)


def kernel(
    groups,
    npts,
    dev,
    sub,
    start,
    fraction,
    grid,
    departed,
    fourier,
    rows,
    moved,
    wide,
    table,
    spectrum,
    start_v,
    frac_v,
    frac_i,
    meta_out,
    meta_in,
    meta_s,
    send1,
    recv1,
    send_m,
    recv_m,
    send2,
    recv2,
    early,
    local,
):
    me = lax.axis_index("lon")
    band = lax.axis_index("lat")
    per = len(rows)
    lats = grid.shape[0]
    halves = grid.shape[1]
    span = halves * BLK

    def to(k):
        return lax.rem(me + k, groups)

    def source(k):
        return lax.rem(me - k + groups, groups)

    barrier = pltpu.get_barrier_semaphore()

    def greet(k, _):
        pl.semaphore_signal(barrier, inc=1, device_id={"lon": to(k)}, device_id_type=MESH)
        return 0

    lax.fori_loop(1, groups, greet, 0)
    inputs = []
    for b in range(halves):
        lanes = pl.ds(b * BLK, BLK)
        inputs.append(pltpu.make_async_copy(start.at[:, lanes], start_v.at[b], early.at[2 * b]))
        inputs.append(pltpu.make_async_copy(fraction.at[:, lanes], frac_v.at[b], early.at[2 * b + 1]))
    for copy in inputs:
        copy.start()
    pl.semaphore_wait(barrier, groups - 1)

    def grid_copy(a, k, peer, place):
        return pltpu.make_async_remote_copy(
            src_ref=grid.at[peer * per + a],
            dst_ref=rows[a].at[pl.ds(place * halves, halves)],
            send_sem=send1.at[a, k],
            recv_sem=recv1.at[a, k],
            device_id={"lon": peer},
            device_id_type=MESH,
        )

    def meta_copy(k, peer, place):
        return pltpu.make_async_remote_copy(
            src_ref=meta_out.at[peer],
            dst_ref=meta_in.at[place],
            send_sem=send_m.at[k],
            recv_sem=recv_m.at[k],
            device_id={"lon": peer},
            device_id_type=MESH,
        )

    def back_copy(a, k, peer, place):
        return pltpu.make_async_remote_copy(
            src_ref=moved.at[a, pl.ds(pl.multiple_of(peer * span, span), span)],
            dst_ref=departed.at[place * per + a],
            send_sem=send2.at[a, k],
            recv_sem=recv2.at[a, k],
            device_id={"lon": peer},
            device_id_type=MESH,
        )

    def send_grid(a):
        def one(k, _):
            grid_copy(a, k, to(k), me).start()
            return 0

        lax.fori_loop(1, groups, one, 0)

    def own_grid(a):
        return pltpu.make_async_copy(
            grid.at[me * per + a],
            rows[a].at[pl.ds(me * halves, halves)],
            local.at[a],
        )

    def own_back(a):
        return pltpu.make_async_copy(
            moved.at[a, pl.ds(pl.multiple_of(me * span, span), span)],
            departed.at[me * per + a],
            local.at[per + a],
        )

    send_grid(0)
    for a in range(per):
        own_grid(a).start()

    for copy in inputs:
        copy.wait()
    frac_i[...] = (frac_v[...].astype(jnp.float32) * FIX).astype(jnp.int32)

    def lay_out(t, _):
        for a in range(per):
            for b in range(halves):
                row = a * halves + b
                block = t * per * halves + row
                base = (dev[block] * halves + sub[block]) * BLK
                own = pl.ds(t * per + a, 1)
                meta_out[t, pl.ds(row, 1), :] = start_v[b, own, :] + base
                meta_out[t, pl.ds(per * halves + row, 1), :] = frac_i[b, own, :]
        return 0

    lax.fori_loop(0, groups, lay_out, 0)
    meta_in[me] = meta_out[me]

    def send_meta(k, _):
        meta_copy(k, to(k), me).start()
        return 0

    lax.fori_loop(1, groups, send_meta, 0)
    for a in range(1, per):
        send_grid(a)

    def take_meta(k, _):
        meta_copy(k, me, source(k)).wait_recv()
        return 0

    lax.fori_loop(1, groups, take_meta, 0)
    meta_copy_s = pltpu.make_async_copy(meta_in, meta_s, local.at[3 * per])
    meta_copy_s.start()
    meta_copy_s.wait()

    node = lax.broadcasted_iota(jnp.int32, (BLK, BLK), 0).astype(jnp.float32)
    lane = lax.broadcasted_iota(jnp.int32, (1, BLK), 1)

    def interpolate(a, length, t, half):
        row = a * halves + half
        j = t * halves + half
        column = meta_in[t, pl.ds(row, 1), :]
        part = meta_in[t, pl.ds(per * halves + row, 1), :].astype(jnp.float32) * (1.0 / FIX)
        begin = (column & (BLK - 1)).astype(jnp.float32)
        live = j * BLK + lane < length
        place = jnp.where(live, begin + 1.0 + part, -1000.0)
        far = jnp.abs(node - place)
        near = 2.0 - far
        inside = (1.0 - far * far) * near * 0.5
        outside = (1.0 - far) * near * (3.0 - far) * (1.0 / 6.0)
        weight = jnp.where(far < 1.0, inside, jnp.where(far < 2.0, outside, 0.0))
        upper = weight.astype(jnp.bfloat16)
        lower = (weight - upper.astype(jnp.float32)).astype(jnp.bfloat16)
        block = meta_s[t, row, 0] >> 7
        values = rows[a][block]
        total = lax.dot_general(
            jnp.concatenate([upper, lower], axis=0),
            jnp.concatenate([values, values], axis=0),
            (((0,), (0,)), ((), ())),
            preferred_element_type=jnp.float32,
        )
        result = total.astype(jnp.bfloat16)
        moved[a, pl.ds(pl.multiple_of(j * BLK, BLK), BLK), :] = result
        pieces = INNER // BLK
        wide[
            pl.ds(pl.multiple_of(lax.rem(j, pieces) * BLK, BLK), BLK),
            pl.ds(pl.multiple_of((j // pieces) * BLK, BLK), BLK),
        ] = result

    def transform(a, length):
        count = jnp.full((8, BLK), length, jnp.int32).astype(jnp.float32)
        size = jnp.broadcast_to(count[:1], (WAVES, BLK))
        inverse = 1.0 / size
        scale = 1.0 / jnp.sqrt(size)
        wave = lax.broadcasted_iota(jnp.int32, (WAVES, BLK), 0).astype(jnp.float32)
        point = lax.broadcasted_iota(jnp.int32, (WAVES, BLK), 1).astype(jnp.float32)
        first = turned(wave * point, size, inverse)
        outer = wide.shape[1] // BLK

        def one(step, _):
            base = step * WAVES
            origin = base.astype(jnp.float32)
            shift = turned(origin * point[:8], count, inverse[:8])
            shift = tuple(jnp.broadcast_to(part[:1], (WAVES, BLK)) for part in shift)
            stride = turned((origin + wave) * float(BLK), size, inverse)
            entry = times(first, shift)
            for piece in range(INNER // BLK):
                lanes = pl.ds(piece * BLK, BLK)
                table[:WAVES, lanes] = entry[0].astype(jnp.bfloat16)
                table[WAVES:, lanes] = entry[1].astype(jnp.bfloat16)
                if piece < INNER // BLK - 1:
                    entry = times(entry, stride)
            jump = stride
            for _ in range((INNER // BLK).bit_length() - 1):
                jump = times(jump, jump)
            product = jnp.dot(table[...], wide[...], preferred_element_type=jnp.float32)

            def of(h):
                part = product[:, h * BLK : (h + 1) * BLK]
                return part[:WAVES], part[WAVES:]

            total = of(outer - 1)
            for h in range(outer - 2, -1, -1):
                ahead = times(total, jump)
                here = of(h)
                total = here[0] + ahead[0], here[1] + ahead[1]
            for part in range(2):
                spectrum[a, part, pl.ds(pl.multiple_of(base, WAVES), WAVES), :] = total[part] * scale
            return 0

        lax.fori_loop(0, MMAX // WAVES, one, 0)

    def result_copy(a):
        return pltpu.make_async_copy(spectrum.at[a], fourier.at[a], local.at[2 * per + a])

    for a in range(per):
        length = npts[band * lats + me * per + a]
        own_grid(a).wait()

        def take_grid(k, _):
            grid_copy(a, k, me, source(k)).wait_recv()
            return 0

        lax.fori_loop(1, groups, take_grid, 0)
        spot = lax.broadcasted_iota(jnp.int32, (BLK, BLK), 0)
        for block in range(LEAST // BLK, rows[a].shape[0]):
            ends = rows[a][block].astype(jnp.float32)
            rows[a][block] = jnp.where(block * BLK + spot < length, ends, 0.0).astype(jnp.bfloat16)

        def answer(k, _):
            t = to(k)
            for half in range(halves):
                interpolate(a, length, t, half)
            back_copy(a, k, t, me).start()
            return 0

        lax.fori_loop(1, groups, answer, 0)
        for half in range(halves):
            interpolate(a, length, me, half)
        own_back(a).start()
        transform(a, length)
        result_copy(a).start()

    for a in range(per):
        own_back(a).wait()
        result_copy(a).wait()

        def finish(k, _):
            grid_copy(a, k, to(k), me).wait_send()
            back_copy(a, k, to(k), me).wait_send()
            back_copy(a, k, me, source(k)).wait_recv()
            return 0

        lax.fori_loop(1, groups, finish, 0)

    def finish_meta(k, _):
        meta_copy(k, to(k), me).wait_send()
        return 0

    lax.fori_loop(1, groups, finish_meta, 0)


def per_device(grid, npts, fraction, start, src_dev, src_sub):
    lats, span, channels = grid.shape
    groups = lax.axis_size("lon")
    per = lats // groups
    points = span * groups
    blocks = lats * span // BLK
    meta = (groups, 2 * per * (span // BLK), BLK)
    smem = pl.BlockSpec(memory_space=pltpu.SMEM)
    anywhere = pl.BlockSpec(memory_space=pl.ANY)
    dma = pltpu.SemaphoreType.DMA
    return pl.pallas_call(
        functools.partial(kernel, groups),
        out_shape=(
            jax.ShapeDtypeStruct(grid.shape, jnp.bfloat16),
            jax.ShapeDtypeStruct((per, 2, MMAX, channels), jnp.float32),
        ),
        in_specs=[smem, smem, smem, anywhere, anywhere, anywhere],
        out_specs=(anywhere, anywhere),
        scratch_shapes=[
            (pltpu.VMEM((points // BLK, BLK, channels), jnp.bfloat16),) * per,
            pltpu.VMEM((per, points, channels), jnp.bfloat16),
            pltpu.VMEM((INNER, points // INNER * channels), jnp.bfloat16),
            pltpu.VMEM((2 * WAVES, INNER), jnp.bfloat16),
            pltpu.VMEM((per, 2, MMAX, channels), jnp.float32),
            pltpu.VMEM((span // BLK, lats, BLK), jnp.int32),
            pltpu.VMEM((span // BLK, lats, BLK), jnp.bfloat16),
            pltpu.VMEM((span // BLK, lats, BLK), jnp.int32),
            pltpu.VMEM(meta, jnp.int32),
            pltpu.VMEM(meta, jnp.int32),
            pltpu.SMEM(meta, jnp.int32),
            dma((per, groups)),
            dma((per, groups)),
            dma((groups,)),
            dma((groups,)),
            dma((per, groups)),
            dma((per, groups)),
            dma((2 * span // BLK,)),
            dma((1 + 3 * per,)),
        ],
        compiler_params=pltpu.CompilerParams(
            collective_id=0, has_side_effects=True, vmem_limit_bytes=56 * 1024 * 1024
        ),
    )(npts, src_dev.reshape(blocks), src_sub.reshape(blocks), start, fraction, grid.reshape(lats, span // BLK, BLK, channels))


def solution(mesh):
    in_specs = (
        P("lat", "lon", None),
        P(),
        P("lat", "lon"),
        P("lat", "lon"),
        P("lat", "lon", None, None),
        P("lat", "lon", None),
    )
    out_specs = (P("lat", "lon", None), P(("lat", "lon"), None, None, None))
    return jax.shard_map(
        per_device, mesh=mesh, in_specs=in_specs, out_specs=out_specs, check_vma=False
    )
```

```python
import functools
import math

import jax
import jax.numpy as jnp
from jax import lax
from jax.experimental import pallas as pl
from jax.experimental.pallas import tpu as pltpu
from jax.sharding import PartitionSpec as P

MMAX = 1280
BLK = 128
WAVES = 128
INNER = 512
LEAST = 3328
FIX = float(1 << 24)
MESH = pl.DeviceIdType.MESH


def unit(turns):
    x = turns * math.pi
    y = x * x
    sine = x * (1.0 + y * (-1 / 6 + y * (1 / 120 + y * (-1 / 5040 + y * (1 / 362880 - y / 39916800)))))
    cosine = 1.0 + y * (
        -1 / 2 + y * (1 / 24 + y * (-1 / 720 + y * (1 / 40320 + y * (-1 / 3628800 + y / 479001600))))
    )
    return 1.0 - 2.0 * sine * sine, -2.0 * sine * cosine


def times(a, b):
    return a[0] * b[0] - a[1] * b[1], a[0] * b[1] + a[1] * b[0]


def turned(product, length, inverse):
    rest = product - jnp.round(product * inverse) * length
    return unit(rest * inverse)


def answer_order(chips):
    release = (0, 24, 33, 41, 61, 56, 47, 38)
    codes = []
    for z in range(chips):
        def dist(c):
            return min((c - z) % chips, (z - c) % chips)
        ranked = sorted(range(chips), key=lambda c: (c == z, min(release[c], release[z]), -dist(c), (c - z) % chips))
        codes.append(sum(c * chips**i for i, c in enumerate(ranked)))
    return codes


def kernel(
    groups,
    npts_hbm,
    dev_hbm,
    sub_hbm,
    start,
    fraction,
    grid,
    departed,
    fourier,
    rows,
    moved,
    wide,
    table,
    npts,
    dev,
    sub,
    start_v,
    frac_v,
    frac_i,
    meta_out,
    meta_in,
    meta_s,
    sent,
    come,
    early,
    local,
):
    me = lax.axis_index("lon")
    band = lax.axis_index("lat")
    per = len(rows)
    lats = grid.shape[0]
    halves = grid.shape[1]
    span = halves * BLK

    def to(k):
        return lax.rem(me + k, groups)

    barrier = pltpu.get_barrier_semaphore()

    def greet(k, _):
        pl.semaphore_signal(barrier, inc=1, device_id={"lon": to(k)}, device_id_type=MESH)
        return 0

    lax.fori_loop(1, groups, greet, 0)
    inputs = [
        pltpu.make_async_copy(far, near, early.at[2 + i])
        for i, (far, near) in enumerate(((npts_hbm, npts), (dev_hbm, dev), (sub_hbm, sub)))
    ]
    for b in range(halves):
        lanes = pl.ds(b * BLK, BLK)
        inputs.append(pltpu.make_async_copy(start.at[:, lanes], start_v.at[b], early.at[0]))
        inputs.append(pltpu.make_async_copy(fraction.at[:, lanes], frac_v.at[b], early.at[1]))
    for copy in inputs:
        copy.start()
    pl.semaphore_wait(barrier, groups - 1)

    def grid_copy(a, peer, place):
        return pltpu.make_async_remote_copy(
            src_ref=grid.at[peer * per + a],
            dst_ref=rows[a].at[pl.ds(place * halves, halves)],
            send_sem=sent.at[0],
            recv_sem=come.at[a],
            device_id={"lon": peer},
            device_id_type=MESH,
        )

    def meta_copy(peer, place):
        return pltpu.make_async_remote_copy(
            src_ref=meta_out.at[peer],
            dst_ref=meta_in.at[place],
            send_sem=sent.at[1],
            recv_sem=come.at[per],
            device_id={"lon": peer},
            device_id_type=MESH,
        )

    def back_copy(a, peer, place):
        return pltpu.make_async_remote_copy(
            src_ref=moved.at[a, pl.ds(pl.multiple_of(peer * span, span), span)],
            dst_ref=departed.at[place * per + a],
            send_sem=sent.at[2 + a],
            recv_sem=come.at[per + 1],
            device_id={"lon": peer},
            device_id_type=MESH,
        )

    def arrived(shape, sem):
        pltpu.make_async_copy(shape, shape, sem).wait()

    def send_grid(a):
        def one(k, _):
            grid_copy(a, to(k), me).start()
            return 0

        lax.fori_loop(1, groups, one, 0)

    def own_grid(a):
        return pltpu.make_async_copy(
            grid.at[me * per + a],
            rows[a].at[pl.ds(me * halves, halves)],
            local.at[a],
        )

    def own_back(a):
        return pltpu.make_async_copy(
            moved.at[a, pl.ds(pl.multiple_of(me * span, span), span)],
            departed.at[me * per + a],
            local.at[per + a],
        )

    send_grid(0)
    for a in range(per):
        own_grid(a).start()

    arrived(start_v, early.at[0])
    arrived(frac_v, early.at[1])
    for copy in inputs[:3]:
        copy.wait()
    frac_i[...] = (frac_v[...].astype(jnp.float32) * FIX).astype(jnp.int32)

    def lay_out(t, _):
        for a in range(per):
            for b in range(halves):
                row = a * halves + b
                block = t * per * halves + row
                base = (dev[block] * halves + sub[block]) * BLK
                own = pl.ds(t * per + a, 1)
                meta_out[t, pl.ds(row, 1), :] = start_v[b, own, :] + base
                meta_out[t, pl.ds(per * halves + row, 1), :] = frac_i[b, own, :]
        return 0

    lax.fori_loop(0, groups, lay_out, 0)
    meta_in[me] = meta_out[me]

    def send_meta(k, _):
        meta_copy(to(k), me).start()
        return 0

    lax.fori_loop(1, groups, send_meta, 0)
    for a in range(1, per):
        send_grid(a)

    arrived(meta_in.at[pl.ds(0, groups - 1)], come.at[per])
    meta_copy_s = pltpu.make_async_copy(meta_in, meta_s, local.at[2 * per])
    meta_copy_s.start()
    meta_copy_s.wait()

    node = lax.broadcasted_iota(jnp.int32, (BLK, BLK), 0).astype(jnp.float32)
    lane = lax.broadcasted_iota(jnp.int32, (1, BLK), 1)

    def interpolate(a, length, t, half):
        row = a * halves + half
        j = t * halves + half
        column = meta_in[t, pl.ds(row, 1), :]
        part = meta_in[t, pl.ds(per * halves + row, 1), :].astype(jnp.float32) * (1.0 / FIX)
        begin = (column & (BLK - 1)).astype(jnp.float32)
        live = j * BLK + lane < length
        place = jnp.where(live, begin + 1.0 + part, -1000.0)
        far = jnp.abs(node - place)
        near = 2.0 - far
        inside = (1.0 - far * far) * near * 0.5
        outside = (1.0 - far) * near * (3.0 - far) * (1.0 / 6.0)
        weight = jnp.where(far < 1.0, inside, jnp.where(far < 2.0, outside, 0.0))
        upper = weight.astype(jnp.bfloat16)
        lower = (weight - upper.astype(jnp.float32)).astype(jnp.bfloat16)
        block = meta_s[t, row, 0] >> 7
        values = rows[a][block]
        total = lax.dot_general(
            jnp.concatenate([upper, lower], axis=0),
            jnp.concatenate([values, values], axis=0),
            (((0,), (0,)), ((), ())),
            preferred_element_type=jnp.float32,
        )
        result = total.astype(jnp.bfloat16)
        moved[a, pl.ds(pl.multiple_of(j * BLK, BLK), BLK), :] = result
        pieces = INNER // BLK
        wide[
            pl.ds(pl.multiple_of(lax.rem(j, pieces) * BLK, BLK), BLK),
            pl.ds(pl.multiple_of((j // pieces) * BLK, BLK), BLK),
        ] = result

    def transform(a, length):
        count = jnp.full((8, BLK), length, jnp.int32).astype(jnp.float32)
        size = jnp.broadcast_to(count[:1], (WAVES, BLK))
        inverse = 1.0 / size
        scale = 1.0 / jnp.sqrt(size)
        wave = lax.broadcasted_iota(jnp.int32, (WAVES, BLK), 0).astype(jnp.float32)
        point = lax.broadcasted_iota(jnp.int32, (WAVES, BLK), 1).astype(jnp.float32)
        first = turned(wave * point, size, inverse)
        outer = wide.shape[1] // BLK

        def one(step, _):
            base = step * WAVES
            origin = base.astype(jnp.float32)
            shift = turned(origin * point[:8], count, inverse[:8])
            shift = tuple(jnp.broadcast_to(part[:1], (WAVES, BLK)) for part in shift)
            stride = turned((origin + wave) * float(BLK), size, inverse)
            entry = times(first, shift)
            for piece in range(INNER // BLK):
                lanes = pl.ds(piece * BLK, BLK)
                table[:WAVES, lanes] = entry[0].astype(jnp.bfloat16)
                table[WAVES:, lanes] = entry[1].astype(jnp.bfloat16)
                if piece < INNER // BLK - 1:
                    entry = times(entry, stride)
            jump = stride
            for _ in range((INNER // BLK).bit_length() - 1):
                jump = times(jump, jump)
            product = jnp.dot(table[...], wide[...], preferred_element_type=jnp.float32)

            def of(h):
                part = product[:, h * BLK : (h + 1) * BLK]
                return part[:WAVES], part[WAVES:]

            total = of(outer - 1)
            for h in range(outer - 2, -1, -1):
                ahead = times(total, jump)
                here = of(h)
                total = here[0] + ahead[0], here[1] + ahead[1]
            for part in range(2):
                fourier[a, part, pl.ds(pl.multiple_of(base, WAVES), WAVES), :] = total[part] * scale
            return 0

        lax.fori_loop(0, MMAX // WAVES, one, 0)

    chips = groups // 2
    z = me // 2
    order = jnp.int32(0)
    for chip, code in enumerate(answer_order(chips)):
        order = jnp.where(z == chip, code, order)

    for a in range(per):
        length = npts[band * lats + me * per + a]
        own_grid(a).wait()

        arrived(rows[a].at[pl.ds(0, (groups - 1) * halves)], come.at[a])
        spot = lax.broadcasted_iota(jnp.int32, (BLK, BLK), 0)
        for block in range(LEAST // BLK, rows[a].shape[0]):
            ends = rows[a][block].astype(jnp.float32)
            rows[a][block] = jnp.where(block * BLK + spot < length, ends, 0.0).astype(jnp.bfloat16)

        def answer(i, code):
            t = (code % chips) * 2 + 1 - i % 2
            for half in range(halves):
                interpolate(a, length, t, half)

            @pl.when(t != me)
            def _():
                back_copy(a, t, me).start()

            @pl.when(t == me)
            def _():
                own_back(a).start()

            return jnp.where(i % 2 == 1, code // chips, code)

        lax.fori_loop(0, groups, answer, order)
        transform(a, length)

    for a in range(per):
        own_back(a).wait()
        arrived(moved.at[a, pl.ds(0, (groups - 1) * span)], sent.at[2 + a])
    arrived(departed.at[pl.ds(0, (groups - 1) * per)], come.at[per + 1])
    arrived(grid.at[pl.ds(0, (groups - 1) * per)], sent.at[0])
    arrived(meta_out.at[pl.ds(0, groups - 1)], sent.at[1])


def settle(departed, fourier, departed_out, fourier_out, sems):
    copies = []
    parts = sems.shape[1]
    for i, (near, far) in enumerate(((departed, departed_out), (fourier, fourier_out))):
        share = near.shape[0] // parts
        for j in range(parts):
            rows = pl.ds(j * share, share)
            copies.append(pltpu.make_async_copy(near.at[rows], far.at[rows], sems.at[i, j]))
    for copy in copies:
        copy.start()
    for copy in copies:
        copy.wait()


def per_device(grid, npts, fraction, start, src_dev, src_sub):
    lats, span, channels = grid.shape
    groups = lax.axis_size("lon")
    per = lats // groups
    points = span * groups
    blocks = lats * span // BLK
    meta = (groups, 2 * per * (span // BLK), BLK)
    dma = pltpu.SemaphoreType.DMA
    outputs = pl.pallas_call(
        functools.partial(kernel, groups),
        out_shape=(
            pltpu.VMEM(grid.shape, jnp.bfloat16),
            pltpu.VMEM((per, 2, MMAX, channels), jnp.float32),
        ),
        in_specs=[pl.BlockSpec(memory_space=pltpu.HBM)] * 6,
        out_specs=(pl.BlockSpec(memory_space=pltpu.VMEM),) * 2,
        scratch_shapes=[
            (pltpu.VMEM((points // BLK, BLK, channels), jnp.bfloat16),) * per,
            pltpu.VMEM((per, points, channels), jnp.bfloat16),
            pltpu.VMEM((INNER, points // INNER * channels), jnp.bfloat16),
            pltpu.VMEM((2 * WAVES, INNER), jnp.bfloat16),
            pltpu.SMEM(npts.shape, jnp.int32),
            pltpu.SMEM((blocks,), jnp.int32),
            pltpu.SMEM((blocks,), jnp.int32),
            pltpu.VMEM((span // BLK, lats, BLK), jnp.int32),
            pltpu.VMEM((span // BLK, lats, BLK), jnp.bfloat16),
            pltpu.VMEM((span // BLK, lats, BLK), jnp.int32),
            pltpu.VMEM(meta, jnp.int32),
            pltpu.VMEM(meta, jnp.int32),
            pltpu.SMEM(meta, jnp.int32),
            dma((2 + per,)),
            dma((2 + per,)),
            dma((5,)),
            dma((1 + 2 * per,)),
        ],
        compiler_params=pltpu.CompilerParams(
            collective_id=0, has_side_effects=True, vmem_limit_bytes=24 * 1024 * 1024
        ),
    )(
        *(
            pltpu.with_memory_space_constraint(array, pltpu.HBM)
            for array in (
                npts,
                src_dev.reshape(blocks),
                src_sub.reshape(blocks),
                start,
                fraction,
                grid.reshape(lats, span // BLK, BLK, channels),
            )
        ),
    )
    vmem = pl.BlockSpec(memory_space=pltpu.VMEM)
    hbm = pl.BlockSpec(memory_space=pltpu.HBM)
    return pl.pallas_call(
        settle,
        out_shape=tuple(pltpu.HBM(array.shape, array.dtype) for array in outputs),
        in_specs=[vmem, vmem],
        out_specs=(hbm, hbm),
        scratch_shapes=[dma((2, per))],
        compiler_params=pltpu.CompilerParams(vmem_limit_bytes=8 * 1024 * 1024),
    )(*(pltpu.with_memory_space_constraint(array, pltpu.VMEM) for array in outputs))


def solution(mesh):
    in_specs = (
        P("lat", "lon", None),
        P(),
        P("lat", "lon"),
        P("lat", "lon"),
        P("lat", "lon", None, None),
        P("lat", "lon", None),
    )
    out_specs = (P("lat", "lon", None), P(("lat", "lon"), None, None, None))
    return jax.shard_map(
        per_device, mesh=mesh, in_specs=in_specs, out_specs=out_specs, check_vma=False
    )
```

```python
import functools
import math

import jax
import jax.numpy as jnp
from jax import lax
from jax.experimental import pallas as pl
from jax.experimental.pallas import tpu as pltpu
from jax.sharding import PartitionSpec as P

MMAX = 1280
BLK = 128
WAVES = 128
INNER = 512
LEAST = 3328
FIX = (1 << 16) - 1
MESH = pl.DeviceIdType.MESH


def unit(turns):
    x = turns * math.pi
    y = x * x
    sine = x * (1.0 + y * (-1 / 6 + y * (1 / 120 + y * (-1 / 5040 + y * (1 / 362880 - y / 39916800)))))
    cosine = 1.0 + y * (
        -1 / 2 + y * (1 / 24 + y * (-1 / 720 + y * (1 / 40320 + y * (-1 / 3628800 + y / 479001600))))
    )
    return 1.0 - 2.0 * sine * sine, -2.0 * sine * cosine


def times(a, b):
    return a[0] * b[0] - a[1] * b[1], a[0] * b[1] + a[1] * b[0]


def turned(product, length, inverse):
    rest = product - jnp.round(product * inverse) * length
    return unit(rest * inverse)


def answer_order(chips):
    ranks = [min(c, chips - c, chips // 4) for c in range(chips)]
    ranks[1:chips // 4 + 1] = [1] * (chips // 4)
    codes = []
    for device in range(2 * chips):
        z, by_reader = device // 2, device % 2 == 1

        def key(c):
            hops = min((c - z) % chips, (z - c) % chips)
            rank = ranks[c] if by_reader else min(ranks[c], ranks[z])
            return c == z, rank, -hops, (c - z) % chips

        codes.append(sum(c * chips**i for i, c in enumerate(sorted(range(chips), key=key))))
    return codes


def kernel(
    groups,
    npts_hbm,
    dev_hbm,
    sub_hbm,
    start,
    fraction,
    grid,
    departed,
    fourier,
    rows,
    moved,
    wide,
    table,
    npts,
    dev,
    sub,
    start_v,
    frac_v,
    frac_i,
    meta_out,
    meta_in,
    meta_s,
    sent,
    come,
    early,
    local,
):
    me = lax.axis_index("lon")
    band = lax.axis_index("lat")
    per = len(rows)
    lats = grid.shape[0]
    halves = grid.shape[1]
    span = halves * BLK

    def to(k):
        return lax.rem(me + k, groups)

    barrier = pltpu.get_barrier_semaphore()

    def greet(k, _):
        pl.semaphore_signal(barrier, inc=1, device_id={"lon": to(k)}, device_id_type=MESH)
        return 0

    lax.fori_loop(1, groups, greet, 0)
    inputs = [
        pltpu.make_async_copy(far, near, early.at[2 + i])
        for i, (far, near) in enumerate(((npts_hbm, npts), (dev_hbm, dev), (sub_hbm, sub)))
    ]
    for b in range(halves):
        lanes = pl.ds(b * BLK, BLK)
        inputs.append(pltpu.make_async_copy(start.at[:, lanes], start_v.at[b], early.at[0]))
        inputs.append(pltpu.make_async_copy(fraction.at[:, lanes], frac_v.at[b], early.at[1]))
    for copy in inputs:
        copy.start()
    pl.semaphore_wait(barrier, groups - 1)

    def grid_copy(a, peer, place):
        return pltpu.make_async_remote_copy(
            src_ref=grid.at[peer * per + a],
            dst_ref=rows[a].at[pl.ds(place * halves, halves)],
            send_sem=sent.at[0],
            recv_sem=come.at[a],
            device_id={"lon": peer},
            device_id_type=MESH,
        )

    def meta_copy(peer, place):
        return pltpu.make_async_remote_copy(
            src_ref=meta_out.at[peer],
            dst_ref=meta_in.at[place],
            send_sem=sent.at[1],
            recv_sem=come.at[per],
            device_id={"lon": peer},
            device_id_type=MESH,
        )

    def back_copy(a, peer, place):
        return pltpu.make_async_remote_copy(
            src_ref=moved.at[a, pl.ds(pl.multiple_of(peer * span, span), span)],
            dst_ref=departed.at[place * per + a],
            send_sem=sent.at[2 + a],
            recv_sem=come.at[per + 1],
            device_id={"lon": peer},
            device_id_type=MESH,
        )

    def arrived(shape, sem):
        pltpu.make_async_copy(shape, shape, sem).wait()

    def send_grid(a):
        def one(k, _):
            grid_copy(a, to(k), me).start()
            return 0

        lax.fori_loop(1, groups, one, 0)

    def own_grid(a):
        return pltpu.make_async_copy(
            grid.at[me * per + a],
            rows[a].at[pl.ds(me * halves, halves)],
            local.at[a],
        )

    def own_back(a):
        return pltpu.make_async_copy(
            moved.at[a, pl.ds(pl.multiple_of(me * span, span), span)],
            departed.at[me * per + a],
            local.at[per + a],
        )

    send_grid(0)
    for a in range(per):
        own_grid(a).start()

    arrived(start_v, early.at[0])
    arrived(frac_v, early.at[1])
    for copy in inputs[:3]:
        copy.wait()
    frac_i[...] = (frac_v[...].astype(jnp.float32) * float(FIX) + 0.5).astype(jnp.int32) & FIX

    def lay_out(t, _):
        for a in range(per):
            for b in range(halves):
                row = a * halves + b
                block = t * per * halves + row
                base = (dev[block] * halves + sub[block]) * BLK
                own = pl.ds(t * per + a, 1)
                meta_out[t, pl.ds(row, 1), :] = (start_v[b, own, :] + base) * (FIX + 1) + frac_i[b, own, :]
        return 0

    lax.fori_loop(0, groups, lay_out, 0)
    meta_in[me] = meta_out[me]

    def send_meta(k, _):
        meta_copy(to(k), me).start()
        return 0

    lax.fori_loop(1, groups, send_meta, 0)
    for a in range(1, per):
        send_grid(a)

    arrived(meta_in.at[pl.ds(0, groups - 1)], come.at[per])
    meta_copy_s = pltpu.make_async_copy(meta_in, meta_s, local.at[2 * per])
    meta_copy_s.start()
    meta_copy_s.wait()

    node = lax.broadcasted_iota(jnp.int32, (BLK, BLK), 0).astype(jnp.float32)
    lane = lax.broadcasted_iota(jnp.int32, (1, BLK), 1)

    def interpolate(a, length, t, half):
        row = a * halves + half
        j = t * halves + half
        word = meta_in[t, pl.ds(row, 1), :]
        part = (word & FIX).astype(jnp.float32) * (1.0 / FIX)
        begin = ((word >> 16) & (BLK - 1)).astype(jnp.float32)
        live = j * BLK + lane < length
        place = jnp.where(live, begin + 1.0 + part, -1000.0)
        far = jnp.abs(node - place)
        near = 2.0 - far
        inside = (1.0 - far * far) * near * 0.5
        outside = (1.0 - far) * near * (3.0 - far) * (1.0 / 6.0)
        weight = jnp.where(far < 1.0, inside, jnp.where(far < 2.0, outside, 0.0))
        upper = weight.astype(jnp.bfloat16)
        lower = (weight - upper.astype(jnp.float32)).astype(jnp.bfloat16)
        block = jnp.clip(meta_s[t, row, 0] >> 23, 0, rows[a].shape[0] - 1)
        values = rows[a][block]
        total = lax.dot_general(
            jnp.concatenate([upper, lower], axis=0),
            jnp.concatenate([values, values], axis=0),
            (((0,), (0,)), ((), ())),
            preferred_element_type=jnp.float32,
        )
        result = total.astype(jnp.bfloat16)
        moved[a, pl.ds(pl.multiple_of(j * BLK, BLK), BLK), :] = result
        pieces = INNER // BLK
        wide[
            pl.ds(pl.multiple_of(lax.rem(j, pieces) * BLK, BLK), BLK),
            pl.ds(pl.multiple_of((j // pieces) * BLK, BLK), BLK),
        ] = result

    def transform(a, length):
        count = jnp.full((8, BLK), length, jnp.int32).astype(jnp.float32)
        size = jnp.broadcast_to(count[:1], (WAVES, BLK))
        inverse = 1.0 / size
        scale = 1.0 / jnp.sqrt(size)
        wave = lax.broadcasted_iota(jnp.int32, (WAVES, BLK), 0).astype(jnp.float32)
        point = lax.broadcasted_iota(jnp.int32, (WAVES, BLK), 1).astype(jnp.float32)
        first = turned(wave * point, size, inverse)
        outer = wide.shape[1] // BLK

        def one(step, _):
            base = step * WAVES
            origin = base.astype(jnp.float32)
            shift = turned(origin * point[:8], count, inverse[:8])
            shift = tuple(jnp.broadcast_to(part[:1], (WAVES, BLK)) for part in shift)
            stride = turned((origin + wave) * float(BLK), size, inverse)
            entry = times(first, shift)
            for piece in range(INNER // BLK):
                lanes = pl.ds(piece * BLK, BLK)
                table[:WAVES, lanes] = entry[0].astype(jnp.bfloat16)
                table[WAVES:, lanes] = entry[1].astype(jnp.bfloat16)
                if piece < INNER // BLK - 1:
                    entry = times(entry, stride)
            jump = stride
            for _ in range((INNER // BLK).bit_length() - 1):
                jump = times(jump, jump)
            product = jnp.dot(table[...], wide[...], preferred_element_type=jnp.float32)

            def of(h):
                part = product[:, h * BLK : (h + 1) * BLK]
                return part[:WAVES], part[WAVES:]

            total = of(outer - 1)
            for h in range(outer - 2, -1, -1):
                ahead = times(total, jump)
                here = of(h)
                total = here[0] + ahead[0], here[1] + ahead[1]
            for part in range(2):
                fourier[a, part, pl.ds(pl.multiple_of(base, WAVES), WAVES), :] = total[part] * scale
            return 0

        lax.fori_loop(0, MMAX // WAVES, one, 0)

    chips = groups // 2
    order = jnp.int32(0)
    for device, code in enumerate(answer_order(chips)):
        order = jnp.where(me == device, code, order)

    for a in range(per):
        length = npts[band * lats + me * per + a]
        own_grid(a).wait()

        arrived(rows[a].at[pl.ds(0, (groups - 1) * halves)], come.at[a])
        spot = lax.broadcasted_iota(jnp.int32, (BLK, BLK), 0)
        for block in range(LEAST // BLK, rows[a].shape[0]):
            ends = rows[a][block].astype(jnp.float32)
            rows[a][block] = jnp.where(block * BLK + spot < length, ends, 0.0).astype(jnp.bfloat16)

        def answer(i, code):
            t = (code % chips) * 2 + lax.rem(i + me, 2)
            for half in range(halves):
                interpolate(a, length, t, half)

            @pl.when(t != me)
            def _():
                back_copy(a, t, me).start()

            @pl.when(t == me)
            def _():
                own_back(a).start()

            return jnp.where(i % 2 == 1, code // chips, code)

        lax.fori_loop(0, groups, answer, order)
        transform(a, length)

    for a in range(per):
        own_back(a).wait()
        arrived(moved.at[a, pl.ds(0, (groups - 1) * span)], sent.at[2 + a])
    arrived(departed.at[pl.ds(0, (groups - 1) * per)], come.at[per + 1])
    arrived(grid.at[pl.ds(0, (groups - 1) * per)], sent.at[0])
    arrived(meta_out.at[pl.ds(0, groups - 1)], sent.at[1])


def settle(departed, fourier, departed_out, fourier_out, sems):
    copies = []
    parts = sems.shape[1]
    for i, (near, far) in enumerate(((departed, departed_out), (fourier, fourier_out))):
        share = near.shape[0] // parts
        for j in range(parts):
            rows = pl.ds(j * share, share)
            copies.append(pltpu.make_async_copy(near.at[rows], far.at[rows], sems.at[i, j]))
    for copy in copies:
        copy.start()
    for copy in copies:
        copy.wait()


def per_device(grid, npts, fraction, start, src_dev, src_sub):
    lats, span, channels = grid.shape
    groups = lax.axis_size("lon")
    per = lats // groups
    points = span * groups
    blocks = lats * span // BLK
    meta = (groups, per * (span // BLK), BLK)
    dma = pltpu.SemaphoreType.DMA
    outputs = pl.pallas_call(
        functools.partial(kernel, groups),
        out_shape=(
            pltpu.VMEM(grid.shape, jnp.bfloat16),
            pltpu.VMEM((per, 2, MMAX, channels), jnp.float32),
        ),
        in_specs=[pl.BlockSpec(memory_space=pltpu.HBM)] * 6,
        out_specs=(pl.BlockSpec(memory_space=pltpu.VMEM),) * 2,
        scratch_shapes=[
            (pltpu.VMEM((points // BLK, BLK, channels), jnp.bfloat16),) * per,
            pltpu.VMEM((per, points, channels), jnp.bfloat16),
            pltpu.VMEM((INNER, points // INNER * channels), jnp.bfloat16),
            pltpu.VMEM((2 * WAVES, INNER), jnp.bfloat16),
            pltpu.SMEM(npts.shape, jnp.int32),
            pltpu.SMEM((blocks,), jnp.int32),
            pltpu.SMEM((blocks,), jnp.int32),
            pltpu.VMEM((span // BLK, lats, BLK), jnp.int32),
            pltpu.VMEM((span // BLK, lats, BLK), jnp.bfloat16),
            pltpu.VMEM((span // BLK, lats, BLK), jnp.int32),
            pltpu.VMEM(meta, jnp.int32),
            pltpu.VMEM(meta, jnp.int32),
            pltpu.SMEM(meta, jnp.int32),
            dma((2 + per,)),
            dma((2 + per,)),
            dma((5,)),
            dma((1 + 2 * per,)),
        ],
        compiler_params=pltpu.CompilerParams(
            collective_id=0, has_side_effects=True, vmem_limit_bytes=24 * 1024 * 1024
        ),
    )(
        *(
            pltpu.with_memory_space_constraint(array, pltpu.HBM)
            for array in (
                npts,
                src_dev.reshape(blocks),
                src_sub.reshape(blocks),
                start,
                fraction,
                grid.reshape(lats, span // BLK, BLK, channels),
            )
        ),
    )
    vmem = pl.BlockSpec(memory_space=pltpu.VMEM)
    hbm = pl.BlockSpec(memory_space=pltpu.HBM)
    return pl.pallas_call(
        settle,
        out_shape=tuple(pltpu.HBM(array.shape, array.dtype) for array in outputs),
        in_specs=[vmem, vmem],
        out_specs=(hbm, hbm),
        scratch_shapes=[dma((2, per))],
        compiler_params=pltpu.CompilerParams(vmem_limit_bytes=8 * 1024 * 1024),
    )(*(pltpu.with_memory_space_constraint(array, pltpu.VMEM) for array in outputs))


def solution(mesh):
    in_specs = (
        P("lat", "lon", None),
        P(),
        P("lat", "lon"),
        P("lat", "lon"),
        P("lat", "lon", None, None),
        P("lat", "lon", None),
    )
    out_specs = (P("lat", "lon", None), P(("lat", "lon"), None, None, None))
    return jax.shard_map(
        per_device, mesh=mesh, in_specs=in_specs, out_specs=out_specs, check_vma=False
    )
```

```python
import functools
import math

import jax
import jax.numpy as jnp
from jax import lax
from jax.experimental import pallas as pl
from jax.experimental.pallas import tpu as pltpu
from jax.sharding import PartitionSpec as P

MMAX = 1280
BLK = 128
WAVES = 128
INNER = 512
LEAST = 3328
FIX = (1 << 16) - 1
MESH = pl.DeviceIdType.MESH


def unit(turns):
    x = turns * math.pi
    y = x * x
    sine = x * (1.0 + y * (-1 / 6 + y * (1 / 120 + y * (-1 / 5040 + y * (1 / 362880 - y / 39916800)))))
    cosine = 1.0 + y * (
        -1 / 2 + y * (1 / 24 + y * (-1 / 720 + y * (1 / 40320 + y * (-1 / 3628800 + y / 479001600))))
    )
    return 1.0 - 2.0 * sine * sine, -2.0 * sine * cosine


def times(a, b):
    return a[0] * b[0] - a[1] * b[1], a[0] * b[1] + a[1] * b[0]


def turned(product, length, inverse):
    rest = product - jnp.round(product * inverse) * length
    return unit(rest * inverse)


def answer_order(chips):
    ranks = [min(c, 3) for c in range(chips)]
    codes = []
    for device in range(2 * chips):
        z, by_reader = device // 2, device % 2 == 1

        def key(c):
            hops = min((c - z) % chips, (z - c) % chips)
            rank = ranks[c] if by_reader else min(ranks[c], ranks[z])
            return c == z, rank, -hops, (c - z) % chips

        codes.append(sum(c * chips**i for i, c in enumerate(sorted(range(chips), key=key))))
    return codes


def kernel(
    groups,
    npts_hbm,
    dev_hbm,
    sub_hbm,
    start,
    fraction,
    grid,
    departed,
    fourier,
    rows,
    moved,
    wide,
    table,
    npts,
    dev,
    sub,
    start_v,
    frac_v,
    frac_i,
    meta_out,
    meta_in,
    meta_s,
    sent,
    come,
    early,
    local,
):
    me = lax.axis_index("lon")
    band = lax.axis_index("lat")
    per = len(rows)
    lats = grid.shape[0]
    halves = grid.shape[1]
    span = halves * BLK

    def to(k):
        return lax.rem(me + k, groups)

    barrier = pltpu.get_barrier_semaphore()

    def greet(k, _):
        pl.semaphore_signal(barrier, inc=1, device_id={"lon": to(k)}, device_id_type=MESH)
        return 0

    lax.fori_loop(1, groups, greet, 0)
    inputs = [
        pltpu.make_async_copy(far, near, early.at[2 + i])
        for i, (far, near) in enumerate(((npts_hbm, npts), (dev_hbm, dev), (sub_hbm, sub)))
    ]
    for b in range(halves):
        lanes = pl.ds(b * BLK, BLK)
        inputs.append(pltpu.make_async_copy(start.at[:, lanes], start_v.at[b], early.at[0]))
        inputs.append(pltpu.make_async_copy(fraction.at[:, lanes], frac_v.at[b], early.at[1]))
    for copy in inputs:
        copy.start()
    pl.semaphore_wait(barrier, groups - 1)

    def grid_copy(a, peer, place):
        return pltpu.make_async_remote_copy(
            src_ref=grid.at[peer * per + a],
            dst_ref=rows[a].at[pl.ds(place * halves, halves)],
            send_sem=sent.at[0],
            recv_sem=come.at[a],
            device_id={"lon": peer},
            device_id_type=MESH,
        )

    def meta_copy(peer, place):
        return pltpu.make_async_remote_copy(
            src_ref=meta_out.at[peer],
            dst_ref=meta_in.at[place],
            send_sem=sent.at[1],
            recv_sem=come.at[per],
            device_id={"lon": peer},
            device_id_type=MESH,
        )

    def back_copy(a, peer, place):
        return pltpu.make_async_remote_copy(
            src_ref=moved.at[a, pl.ds(pl.multiple_of(peer * span, span), span)],
            dst_ref=departed.at[place * per + a],
            send_sem=sent.at[2 + a],
            recv_sem=come.at[per + 1],
            device_id={"lon": peer},
            device_id_type=MESH,
        )

    def arrived(shape, sem):
        pltpu.make_async_copy(shape, shape, sem).wait()

    def send_grid(a):
        def one(k, _):
            grid_copy(a, to(k), me).start()
            return 0

        lax.fori_loop(1, groups, one, 0)

    def own_grid(a):
        return pltpu.make_async_copy(
            grid.at[me * per + a],
            rows[a].at[pl.ds(me * halves, halves)],
            local.at[a],
        )

    def own_back(a):
        return pltpu.make_async_copy(
            moved.at[a, pl.ds(pl.multiple_of(me * span, span), span)],
            departed.at[me * per + a],
            local.at[per + a],
        )

    send_grid(0)
    for a in range(per):
        own_grid(a).start()

    arrived(start_v, early.at[0])
    arrived(frac_v, early.at[1])
    for copy in inputs[:3]:
        copy.wait()
    frac_i[...] = (frac_v[...].astype(jnp.float32) * float(FIX) + 0.5).astype(jnp.int32) & FIX

    def lay_out(t, _):
        for a in range(per):
            for b in range(halves):
                row = a * halves + b
                block = t * per * halves + row
                base = (dev[block] * halves + sub[block]) * BLK
                own = pl.ds(t * per + a, 1)
                meta_out[t, pl.ds(row, 1), :] = (start_v[b, own, :] + base) * (FIX + 1) + frac_i[b, own, :]
        return 0

    lax.fori_loop(0, groups, lay_out, 0)
    meta_in[me] = meta_out[me]

    def send_meta(k, _):
        meta_copy(to(k), me).start()
        return 0

    lax.fori_loop(1, groups, send_meta, 0)
    for a in range(1, per):
        send_grid(a)

    arrived(meta_in.at[pl.ds(0, groups - 1)], come.at[per])
    meta_copy_s = pltpu.make_async_copy(meta_in, meta_s, local.at[2 * per])
    meta_copy_s.start()
    meta_copy_s.wait()

    node = lax.broadcasted_iota(jnp.int32, (BLK, BLK), 0).astype(jnp.float32)
    lane = lax.broadcasted_iota(jnp.int32, (1, BLK), 1)

    def interpolate(a, length, t, half):
        row = a * halves + half
        j = t * halves + half
        word = meta_in[t, pl.ds(row, 1), :]
        part = (word & FIX).astype(jnp.float32) * (1.0 / FIX)
        begin = ((word >> 16) & (BLK - 1)).astype(jnp.float32)
        live = j * BLK + lane < length
        place = jnp.where(live, begin + 1.0 + part, -1000.0)
        far = jnp.abs(node - place)
        near = 2.0 - far
        inside = (1.0 - far * far) * near * 0.5
        outside = (1.0 - far) * near * (3.0 - far) * (1.0 / 6.0)
        weight = jnp.where(far < 1.0, inside, jnp.where(far < 2.0, outside, 0.0))
        upper = weight.astype(jnp.bfloat16)
        lower = (weight - upper.astype(jnp.float32)).astype(jnp.bfloat16)
        block = jnp.clip(meta_s[t, row, 0] >> 23, 0, rows[a].shape[0] - 1)
        values = rows[a][block]
        total = lax.dot_general(
            jnp.concatenate([upper, lower], axis=0),
            jnp.concatenate([values, values], axis=0),
            (((0,), (0,)), ((), ())),
            preferred_element_type=jnp.float32,
        )
        result = total.astype(jnp.bfloat16)
        moved[a, pl.ds(pl.multiple_of(j * BLK, BLK), BLK), :] = result
        pieces = INNER // BLK
        wide[
            pl.ds(pl.multiple_of(lax.rem(j, pieces) * BLK, BLK), BLK),
            pl.ds(pl.multiple_of((j // pieces) * BLK, BLK), BLK),
        ] = result

    def transform(a, length):
        count = jnp.full((8, BLK), length, jnp.int32).astype(jnp.float32)
        size = jnp.broadcast_to(count[:1], (WAVES, BLK))
        inverse = 1.0 / size
        scale = 1.0 / jnp.sqrt(size)
        wave = lax.broadcasted_iota(jnp.int32, (WAVES, BLK), 0).astype(jnp.float32)
        point = lax.broadcasted_iota(jnp.int32, (WAVES, BLK), 1).astype(jnp.float32)
        first = turned(wave * point, size, inverse)
        outer = wide.shape[1] // BLK

        def one(step, _):
            base = step * WAVES
            origin = base.astype(jnp.float32)
            shift = turned(origin * point[:8], count, inverse[:8])
            shift = tuple(jnp.broadcast_to(part[:1], (WAVES, BLK)) for part in shift)
            stride = turned((origin + wave) * float(BLK), size, inverse)
            entry = times(first, shift)
            for piece in range(INNER // BLK):
                lanes = pl.ds(piece * BLK, BLK)
                table[:WAVES, lanes] = entry[0].astype(jnp.bfloat16)
                table[WAVES:, lanes] = entry[1].astype(jnp.bfloat16)
                if piece < INNER // BLK - 1:
                    entry = times(entry, stride)
            jump = stride
            for _ in range((INNER // BLK).bit_length() - 1):
                jump = times(jump, jump)
            product = jnp.dot(table[...], wide[...], preferred_element_type=jnp.float32)

            def of(h):
                part = product[:, h * BLK : (h + 1) * BLK]
                return part[:WAVES], part[WAVES:]

            total = of(outer - 1)
            for h in range(outer - 2, -1, -1):
                ahead = times(total, jump)
                here = of(h)
                total = here[0] + ahead[0], here[1] + ahead[1]
            for part in range(2):
                fourier[a, part, pl.ds(pl.multiple_of(base, WAVES), WAVES), :] = total[part] * scale
            return 0

        lax.fori_loop(0, MMAX // WAVES, one, 0)

    chips = groups // 2
    order = jnp.int32(0)
    for device, code in enumerate(answer_order(chips)):
        order = jnp.where(me == device, code, order)

    for a in range(per):
        length = npts[band * lats + me * per + a]
        own_grid(a).wait()

        arrived(rows[a].at[pl.ds(0, (groups - 1) * halves)], come.at[a])
        spot = lax.broadcasted_iota(jnp.int32, (BLK, BLK), 0)
        for block in range(LEAST // BLK, rows[a].shape[0]):
            ends = rows[a][block].astype(jnp.float32)
            rows[a][block] = jnp.where(block * BLK + spot < length, ends, 0.0).astype(jnp.bfloat16)

        def answer(i, code):
            t = (code % chips) * 2 + lax.rem(i + me, 2)
            for half in range(halves):
                interpolate(a, length, t, half)

            @pl.when(t != me)
            def _():
                back_copy(a, t, me).start()

            @pl.when(t == me)
            def _():
                own_back(a).start()

            return jnp.where(i % 2 == 1, code // chips, code)

        lax.fori_loop(0, groups, answer, order)
        transform(a, length)

    for a in range(per):
        own_back(a).wait()
        arrived(moved.at[a, pl.ds(0, (groups - 1) * span)], sent.at[2 + a])
    arrived(departed.at[pl.ds(0, (groups - 1) * per)], come.at[per + 1])
    arrived(grid.at[pl.ds(0, (groups - 1) * per)], sent.at[0])
    arrived(meta_out.at[pl.ds(0, groups - 1)], sent.at[1])


def settle(departed, fourier, departed_out, fourier_out, sems):
    copies = []
    parts = sems.shape[1]
    for i, (near, far) in enumerate(((departed, departed_out), (fourier, fourier_out))):
        share = near.shape[0] // parts
        for j in range(parts):
            rows = pl.ds(j * share, share)
            copies.append(pltpu.make_async_copy(near.at[rows], far.at[rows], sems.at[i, j]))
    for copy in copies:
        copy.start()
    for copy in copies:
        copy.wait()


def per_device(grid, npts, fraction, start, src_dev, src_sub):
    lats, span, channels = grid.shape
    groups = lax.axis_size("lon")
    per = lats // groups
    points = span * groups
    blocks = lats * span // BLK
    meta = (groups, per * (span // BLK), BLK)
    dma = pltpu.SemaphoreType.DMA
    outputs = pl.pallas_call(
        functools.partial(kernel, groups),
        out_shape=(
            pltpu.VMEM(grid.shape, jnp.bfloat16),
            pltpu.VMEM((per, 2, MMAX, channels), jnp.float32),
        ),
        in_specs=[pl.BlockSpec(memory_space=pltpu.HBM)] * 6,
        out_specs=(pl.BlockSpec(memory_space=pltpu.VMEM),) * 2,
        scratch_shapes=[
            (pltpu.VMEM((points // BLK, BLK, channels), jnp.bfloat16),) * per,
            pltpu.VMEM((per, points, channels), jnp.bfloat16),
            pltpu.VMEM((INNER, points // INNER * channels), jnp.bfloat16),
            pltpu.VMEM((2 * WAVES, INNER), jnp.bfloat16),
            pltpu.SMEM(npts.shape, jnp.int32),
            pltpu.SMEM((blocks,), jnp.int32),
            pltpu.SMEM((blocks,), jnp.int32),
            pltpu.VMEM((span // BLK, lats, BLK), jnp.int32),
            pltpu.VMEM((span // BLK, lats, BLK), jnp.bfloat16),
            pltpu.VMEM((span // BLK, lats, BLK), jnp.int32),
            pltpu.VMEM(meta, jnp.int32),
            pltpu.VMEM(meta, jnp.int32),
            pltpu.SMEM(meta, jnp.int32),
            dma((2 + per,)),
            dma((2 + per,)),
            dma((5,)),
            dma((1 + 2 * per,)),
        ],
        compiler_params=pltpu.CompilerParams(
            collective_id=0, has_side_effects=True, vmem_limit_bytes=24 * 1024 * 1024
        ),
    )(
        *(
            pltpu.with_memory_space_constraint(array, pltpu.HBM)
            for array in (
                npts,
                src_dev.reshape(blocks),
                src_sub.reshape(blocks),
                start,
                fraction,
                grid.reshape(lats, span // BLK, BLK, channels),
            )
        ),
    )
    vmem = pl.BlockSpec(memory_space=pltpu.VMEM)
    hbm = pl.BlockSpec(memory_space=pltpu.HBM)
    return pl.pallas_call(
        settle,
        out_shape=tuple(pltpu.HBM(array.shape, array.dtype) for array in outputs),
        in_specs=[vmem, vmem],
        out_specs=(hbm, hbm),
        scratch_shapes=[dma((2, per))],
        compiler_params=pltpu.CompilerParams(vmem_limit_bytes=8 * 1024 * 1024),
    )(*(pltpu.with_memory_space_constraint(array, pltpu.VMEM) for array in outputs))


def solution(mesh):
    in_specs = (
        P("lat", "lon", None),
        P(),
        P("lat", "lon"),
        P("lat", "lon"),
        P("lat", "lon", None, None),
        P("lat", "lon", None),
    )
    out_specs = (P("lat", "lon", None), P(("lat", "lon"), None, None, None))
    return jax.shard_map(
        per_device, mesh=mesh, in_specs=in_specs, out_specs=out_specs, check_vma=False
    )
```

```python
import functools
import math

import jax
import jax.numpy as jnp
from jax import lax
from jax.experimental import pallas as pl
from jax.experimental.pallas import tpu as pltpu
from jax.sharding import PartitionSpec as P

MMAX = 1280
BLK = 128
WAVES = 128
INNER = 512
LEAST = 3328
FIX = (1 << 16) - 1
MESH = pl.DeviceIdType.MESH


def unit(turns):
    x = turns * math.pi
    y = x * x
    sine = x * (1.0 + y * (-1 / 6 + y * (1 / 120 + y * (-1 / 5040 + y * (1 / 362880 - y / 39916800)))))
    cosine = 1.0 + y * (
        -1 / 2 + y * (1 / 24 + y * (-1 / 720 + y * (1 / 40320 + y * (-1 / 3628800 + y / 479001600))))
    )
    return 1.0 - 2.0 * sine * sine, -2.0 * sine * cosine


def times(a, b):
    return a[0] * b[0] - a[1] * b[1], a[0] * b[1] + a[1] * b[0]


def turned(product, length, inverse):
    rest = product - jnp.round(product * inverse) * length
    return unit(rest * inverse)


def answer_order(chips):
    ranks = [0, 1, 2, 3, 3, 3, 3, 2]
    codes = []
    for device in range(2 * chips):
        z, by_reader = device // 2, device % 2 == 1

        def key(c):
            hops = min((c - z) % chips, (z - c) % chips)
            rank = ranks[c] if by_reader else min(ranks[c], ranks[z])
            return c == z, rank, -hops, (c - z) % chips

        codes.append(sum(c * chips**i for i, c in enumerate(sorted(range(chips), key=key))))
    return codes


def kernel(
    groups,
    npts_hbm,
    dev_hbm,
    sub_hbm,
    start,
    fraction,
    grid,
    departed,
    fourier,
    rows,
    moved,
    wide,
    table,
    npts,
    dev,
    sub,
    start_v,
    frac_v,
    frac_i,
    meta_out,
    meta_in,
    meta_s,
    sent,
    come,
    early,
    local,
):
    me = lax.axis_index("lon")
    band = lax.axis_index("lat")
    per = len(rows)
    lats = grid.shape[0]
    halves = grid.shape[1]
    span = halves * BLK

    def to(k):
        return lax.rem(me + k, groups)

    barrier = pltpu.get_barrier_semaphore()

    def greet(k, _):
        pl.semaphore_signal(barrier, inc=1, device_id={"lon": to(k)}, device_id_type=MESH)
        return 0

    lax.fori_loop(1, groups, greet, 0)
    inputs = [
        pltpu.make_async_copy(far, near, early.at[2 + i])
        for i, (far, near) in enumerate(((npts_hbm, npts), (dev_hbm, dev), (sub_hbm, sub)))
    ]
    for b in range(halves):
        lanes = pl.ds(b * BLK, BLK)
        inputs.append(pltpu.make_async_copy(start.at[:, lanes], start_v.at[b], early.at[0]))
        inputs.append(pltpu.make_async_copy(fraction.at[:, lanes], frac_v.at[b], early.at[1]))
    for copy in inputs:
        copy.start()
    pl.semaphore_wait(barrier, groups - 1)

    def grid_copy(a, peer, place):
        return pltpu.make_async_remote_copy(
            src_ref=grid.at[peer * per + a],
            dst_ref=rows[a].at[pl.ds(place * halves, halves)],
            send_sem=sent.at[0],
            recv_sem=come.at[a],
            device_id={"lon": peer},
            device_id_type=MESH,
        )

    def meta_copy(peer, place):
        return pltpu.make_async_remote_copy(
            src_ref=meta_out.at[peer],
            dst_ref=meta_in.at[place],
            send_sem=sent.at[1],
            recv_sem=come.at[per],
            device_id={"lon": peer},
            device_id_type=MESH,
        )

    def back_copy(a, peer, place):
        return pltpu.make_async_remote_copy(
            src_ref=moved.at[a, pl.ds(pl.multiple_of(peer * span, span), span)],
            dst_ref=departed.at[place * per + a],
            send_sem=sent.at[2 + a],
            recv_sem=come.at[per + 1],
            device_id={"lon": peer},
            device_id_type=MESH,
        )

    def arrived(shape, sem):
        pltpu.make_async_copy(shape, shape, sem).wait()

    def send_grid(a):
        def one(k, _):
            grid_copy(a, to(k), me).start()
            return 0

        lax.fori_loop(1, groups, one, 0)

    def own_grid(a):
        return pltpu.make_async_copy(
            grid.at[me * per + a],
            rows[a].at[pl.ds(me * halves, halves)],
            local.at[a],
        )

    def own_back(a):
        return pltpu.make_async_copy(
            moved.at[a, pl.ds(pl.multiple_of(me * span, span), span)],
            departed.at[me * per + a],
            local.at[per + a],
        )

    send_grid(0)
    for a in range(per):
        own_grid(a).start()

    arrived(start_v, early.at[0])
    arrived(frac_v, early.at[1])
    for copy in inputs[:3]:
        copy.wait()
    frac_i[...] = (frac_v[...].astype(jnp.float32) * float(FIX) + 0.5).astype(jnp.int32) & FIX

    def lay_out(t, _):
        for a in range(per):
            for b in range(halves):
                row = a * halves + b
                block = t * per * halves + row
                base = (dev[block] * halves + sub[block]) * BLK
                own = pl.ds(t * per + a, 1)
                meta_out[t, pl.ds(row, 1), :] = (start_v[b, own, :] + base) * (FIX + 1) + frac_i[b, own, :]
        return 0

    lax.fori_loop(0, groups, lay_out, 0)
    meta_in[me] = meta_out[me]

    def send_meta(k, _):
        meta_copy(to(k), me).start()
        return 0

    lax.fori_loop(1, groups, send_meta, 0)
    for a in range(1, per):
        send_grid(a)

    arrived(meta_in.at[pl.ds(0, groups - 1)], come.at[per])
    meta_copy_s = pltpu.make_async_copy(meta_in, meta_s, local.at[2 * per])
    meta_copy_s.start()
    meta_copy_s.wait()

    node = lax.broadcasted_iota(jnp.int32, (BLK, BLK), 0).astype(jnp.float32)
    lane = lax.broadcasted_iota(jnp.int32, (1, BLK), 1)

    def interpolate(a, length, t, half):
        row = a * halves + half
        j = t * halves + half
        word = meta_in[t, pl.ds(row, 1), :]
        part = (word & FIX).astype(jnp.float32) * (1.0 / FIX)
        begin = ((word >> 16) & (BLK - 1)).astype(jnp.float32)
        live = j * BLK + lane < length
        place = jnp.where(live, begin + 1.0 + part, -1000.0)
        far = jnp.abs(node - place)
        near = 2.0 - far
        inside = (1.0 - far * far) * near * 0.5
        outside = (1.0 - far) * near * (3.0 - far) * (1.0 / 6.0)
        weight = jnp.where(far < 1.0, inside, jnp.where(far < 2.0, outside, 0.0))
        upper = weight.astype(jnp.bfloat16)
        lower = (weight - upper.astype(jnp.float32)).astype(jnp.bfloat16)
        block = jnp.clip(meta_s[t, row, 0] >> 23, 0, rows[a].shape[0] - 1)
        values = rows[a][block]
        total = lax.dot_general(
            jnp.concatenate([upper, lower], axis=0),
            jnp.concatenate([values, values], axis=0),
            (((0,), (0,)), ((), ())),
            preferred_element_type=jnp.float32,
        )
        result = total.astype(jnp.bfloat16)
        moved[a, pl.ds(pl.multiple_of(j * BLK, BLK), BLK), :] = result
        pieces = INNER // BLK
        wide[
            pl.ds(pl.multiple_of(lax.rem(j, pieces) * BLK, BLK), BLK),
            pl.ds(pl.multiple_of((j // pieces) * BLK, BLK), BLK),
        ] = result

    def transform(a, length):
        count = jnp.full((8, BLK), length, jnp.int32).astype(jnp.float32)
        size = jnp.broadcast_to(count[:1], (WAVES, BLK))
        inverse = 1.0 / size
        scale = 1.0 / jnp.sqrt(size)
        wave = lax.broadcasted_iota(jnp.int32, (WAVES, BLK), 0).astype(jnp.float32)
        point = lax.broadcasted_iota(jnp.int32, (WAVES, BLK), 1).astype(jnp.float32)
        first = turned(wave * point, size, inverse)
        outer = wide.shape[1] // BLK

        def one(step, _):
            base = step * WAVES
            origin = base.astype(jnp.float32)
            shift = turned(origin * point[:8], count, inverse[:8])
            shift = tuple(jnp.broadcast_to(part[:1], (WAVES, BLK)) for part in shift)
            stride = turned((origin + wave) * float(BLK), size, inverse)
            entry = times(first, shift)
            for piece in range(INNER // BLK):
                lanes = pl.ds(piece * BLK, BLK)
                table[:WAVES, lanes] = entry[0].astype(jnp.bfloat16)
                table[WAVES:, lanes] = entry[1].astype(jnp.bfloat16)
                if piece < INNER // BLK - 1:
                    entry = times(entry, stride)
            jump = stride
            for _ in range((INNER // BLK).bit_length() - 1):
                jump = times(jump, jump)
            product = jnp.dot(table[...], wide[...], preferred_element_type=jnp.float32)

            def of(h):
                part = product[:, h * BLK : (h + 1) * BLK]
                return part[:WAVES], part[WAVES:]

            total = of(outer - 1)
            for h in range(outer - 2, -1, -1):
                ahead = times(total, jump)
                here = of(h)
                total = here[0] + ahead[0], here[1] + ahead[1]
            for part in range(2):
                fourier[a, part, pl.ds(pl.multiple_of(base, WAVES), WAVES), :] = total[part] * scale
            return 0

        lax.fori_loop(0, MMAX // WAVES, one, 0)

    chips = groups // 2
    order = jnp.int32(0)
    for device, code in enumerate(answer_order(chips)):
        order = jnp.where(me == device, code, order)

    for a in range(per):
        length = npts[band * lats + me * per + a]
        own_grid(a).wait()

        arrived(rows[a].at[pl.ds(0, (groups - 1) * halves)], come.at[a])
        spot = lax.broadcasted_iota(jnp.int32, (BLK, BLK), 0)
        for block in range(LEAST // BLK, rows[a].shape[0]):
            ends = rows[a][block].astype(jnp.float32)
            rows[a][block] = jnp.where(block * BLK + spot < length, ends, 0.0).astype(jnp.bfloat16)

        def answer(i, code):
            t = (code % chips) * 2 + lax.rem(i + me, 2)
            for half in range(halves):
                interpolate(a, length, t, half)

            @pl.when(t != me)
            def _():
                back_copy(a, t, me).start()

            @pl.when(t == me)
            def _():
                own_back(a).start()

            return jnp.where(i % 2 == 1, code // chips, code)

        lax.fori_loop(0, groups, answer, order)
        transform(a, length)

    for a in range(per):
        own_back(a).wait()
        arrived(moved.at[a, pl.ds(0, (groups - 1) * span)], sent.at[2 + a])
    arrived(departed.at[pl.ds(0, (groups - 1) * per)], come.at[per + 1])
    arrived(grid.at[pl.ds(0, (groups - 1) * per)], sent.at[0])
    arrived(meta_out.at[pl.ds(0, groups - 1)], sent.at[1])


def settle(departed, fourier, departed_out, fourier_out, sems):
    copies = []
    parts = sems.shape[1]
    for i, (near, far) in enumerate(((departed, departed_out), (fourier, fourier_out))):
        share = near.shape[0] // parts
        for j in range(parts):
            rows = pl.ds(j * share, share)
            copies.append(pltpu.make_async_copy(near.at[rows], far.at[rows], sems.at[i, j]))
    for copy in copies:
        copy.start()
    for copy in copies:
        copy.wait()


def per_device(grid, npts, fraction, start, src_dev, src_sub):
    lats, span, channels = grid.shape
    groups = lax.axis_size("lon")
    per = lats // groups
    points = span * groups
    blocks = lats * span // BLK
    meta = (groups, per * (span // BLK), BLK)
    dma = pltpu.SemaphoreType.DMA
    outputs = pl.pallas_call(
        functools.partial(kernel, groups),
        out_shape=(
            pltpu.VMEM(grid.shape, jnp.bfloat16),
            pltpu.VMEM((per, 2, MMAX, channels), jnp.float32),
        ),
        in_specs=[pl.BlockSpec(memory_space=pltpu.HBM)] * 6,
        out_specs=(pl.BlockSpec(memory_space=pltpu.VMEM),) * 2,
        scratch_shapes=[
            (pltpu.VMEM((points // BLK, BLK, channels), jnp.bfloat16),) * per,
            pltpu.VMEM((per, points, channels), jnp.bfloat16),
            pltpu.VMEM((INNER, points // INNER * channels), jnp.bfloat16),
            pltpu.VMEM((2 * WAVES, INNER), jnp.bfloat16),
            pltpu.SMEM(npts.shape, jnp.int32),
            pltpu.SMEM((blocks,), jnp.int32),
            pltpu.SMEM((blocks,), jnp.int32),
            pltpu.VMEM((span // BLK, lats, BLK), jnp.int32),
            pltpu.VMEM((span // BLK, lats, BLK), jnp.bfloat16),
            pltpu.VMEM((span // BLK, lats, BLK), jnp.int32),
            pltpu.VMEM(meta, jnp.int32),
            pltpu.VMEM(meta, jnp.int32),
            pltpu.SMEM(meta, jnp.int32),
            dma((2 + per,)),
            dma((2 + per,)),
            dma((5,)),
            dma((1 + 2 * per,)),
        ],
        compiler_params=pltpu.CompilerParams(
            collective_id=0, has_side_effects=True, vmem_limit_bytes=24 * 1024 * 1024
        ),
    )(
        *(
            pltpu.with_memory_space_constraint(array, pltpu.HBM)
            for array in (
                npts,
                src_dev.reshape(blocks),
                src_sub.reshape(blocks),
                start,
                fraction,
                grid.reshape(lats, span // BLK, BLK, channels),
            )
        ),
    )
    vmem = pl.BlockSpec(memory_space=pltpu.VMEM)
    hbm = pl.BlockSpec(memory_space=pltpu.HBM)
    return pl.pallas_call(
        settle,
        out_shape=tuple(pltpu.HBM(array.shape, array.dtype) for array in outputs),
        in_specs=[vmem, vmem],
        out_specs=(hbm, hbm),
        scratch_shapes=[dma((2, per))],
        compiler_params=pltpu.CompilerParams(vmem_limit_bytes=8 * 1024 * 1024),
    )(*(pltpu.with_memory_space_constraint(array, pltpu.VMEM) for array in outputs))


def solution(mesh):
    in_specs = (
        P("lat", "lon", None),
        P(),
        P("lat", "lon"),
        P("lat", "lon"),
        P("lat", "lon", None, None),
        P("lat", "lon", None),
    )
    out_specs = (P("lat", "lon", None), P(("lat", "lon"), None, None, None))
    return jax.shard_map(
        per_device, mesh=mesh, in_specs=in_specs, out_specs=out_specs, check_vma=False
    )
```
